32 devices in a mesh: tower: 2 (over core), shard: 16 (over z, y, x).
Axes of the slice: x: 2, y: 2, z: 4, core: 2. Of those that a mesh axis runs over, the one named last changes fastest.
Arguments:
- hidden: bfloat16 [2, 8192, 4096], P('tower', 'shard'), may hold values from -6 to 6
- head: float32 [2, 4096, 512], P('tower'), may hold values from -0.09375 to 0.09375
- pos_local: int32 [8192], P('shard'), may hold values from 0 to 511
- requests: int32 [16, 16, 4], P(None, 'shard'), may hold values from 0 to 511, as said below
- neg_slot: int32 [8192, 8], P('shard'), may hold values from 0 to 63
Outputs:
- head_grad: float32 [2, 4096, 512], P('tower', 'shard')
The draws below stay inside these ranges and needn't reach their ends.
Inputs may be any that keep to these rules, and one draw needn't show every extreme that they name: requests[s, o, :] names 4 different rows of owner o.
All inputs are finite; a program needn't handle non-finite values.
Results may differ from the reference program's by a relative error of at most 0.0004.
The reference program's roundings to bfloat16 on the way count: a program that leaves them out, or rounds other values in their place, can miss the bound.
Values may be sent and summed in bfloat16 or wider, within the bound.
A program may use at most 128 MiB of HBM per device.

```python
import math
import jax
import jax.numpy as jnp
import numpy as np
from jax import lax

D = 4096
PROJ = 512
ROWS = 512
NEG = 8
CAP = 4
SHARDS = 16
ROWS_ALL = 8192


def draw_requests(key, part):
    keys = jax.random.split(jax.random.fold_in(key, 17), SHARDS * SHARDS)

    def one_pair(pair_key):
        return jax.random.permutation(pair_key, ROWS)[:CAP]
    chosen = jax.vmap(one_pair)(keys)
    return chosen.reshape(SHARDS, SHARDS, CAP).astype(jnp.int32)


def touch_ends(result, rng, least, high):
    longest = result.shape.index(max(result.shape))
    spots = []
    for shift in (0, 1):
        where = [jax.random.randint(jax.random.fold_in(rng, axis), (), 0, length) for axis, length in enumerate(result.shape)]
        where[longest] = (where[longest] + shift) % result.shape[longest]
        spots.append(tuple(where))
    return result.at[spots[0]].set(least).at[spots[1]].set(high)


def strengthened(array, stream_key, source, target, parts, factor):
    owner, partner = [(jnp.arange(array.shape[dim]) // (array.shape[dim] // parts)).reshape([-1 if axis == dim else 1 for axis in range(array.ndim)]) for dim in (source, target)]
    chosen = jax.random.permutation(stream_key, parts)[partner]
    strong = (owner == chosen) | (owner == (partner + parts // 2) % parts)
    return jnp.where(strong, factor * array, array)


def block_levels(rng, shape, cuts, low, high):
    level, own = 1.0, jax.random.fold_in(rng, 6)
    for axis_at, parts in cuts:
        draws = jnp.exp(jax.random.uniform(jax.random.fold_in(own, axis_at), (parts,), jnp.float32, low / len(cuts), high / len(cuts)))
        level = level * jnp.repeat(draws, shape[axis_at] // parts).reshape([-1 if axis == axis_at else 1 for axis in range(len(shape))])
    return level


def rank_bounds(number_of, lean):
    loads = [(1 << 20) // math.isqrt(rank ** lean) + 1 for rank in range(1, number_of + 1)]
    width = 1 + sum(loads) // (1 << 30)
    return np.cumsum(np.array([max(1, weight // width) for weight in loads]))


def ranked_ids(own_key, dims, count, slope):
    table = rank_bounds(count, slope)
    pick = jax.random.randint(jax.random.fold_in(own_key, 1), dims, 0, int(table[count - 1]))
    rank = jnp.searchsorted(jnp.asarray(table, jnp.int32), pick, side="right")
    return jax.random.permutation(jax.random.fold_in(own_key, 2), count)[rank].astype(jnp.int32)


def noise(rng, shape, width, bound, cuts=(), kind=jnp.bfloat16):
    drawn = width * jax.random.normal(rng, shape, jnp.float32)
    if cuts:
        drawn = drawn * block_levels(rng, shape, cuts, -0.22, 0.18)
    return jnp.clip(drawn, -bound, bound).astype(kind)


def bell_draw_with(key, extent, scale, bound, cuts, heavy, held_as=jnp.bfloat16):
    result = scale * jax.random.normal(key, extent, jnp.float32)
    if cuts:
        result = result * block_levels(key, extent, cuts, -0.22, 0.18)
    return jnp.clip(strengthened(result, jax.random.fold_in(key, 3), *heavy), -bound, bound).astype(held_as)


def setup_inputs(seed: int = 0) -> dict:
    splits = jax.random.split(jax.random.key(seed), 6)
    return {
        "hidden": bell_draw_with(splits[0], (2, ROWS_ALL, D), 1.0, 6.0, ((0, 2), (1, 16)), (1, 2, 16, 2.0)),
        "head": noise(splits[1], (2, D, PROJ), D ** -0.5, 0.09375, ((0, 2),), jnp.float32),
        "pos_local": touch_ends(jax.random.randint(splits[2], (ROWS_ALL,), 0, ROWS), jax.random.fold_in(splits[2], 1), 0, ROWS - 1).astype(jnp.int32),
        "requests": draw_requests(jax.random.fold_in(splits[5], 71), 0),
        "neg_slot": touch_ends(ranked_ids(splits[4], (ROWS_ALL, NEG), SHARDS * CAP, 2), jax.random.fold_in(splits[4], 3), 0, (SHARDS * CAP) - 1).astype(jnp.int32),
    }


logit_divisor = 0.05
epsilon = 1e-06

def project(hidden_rows, weights):
    embedded = jnp.dot(hidden_rows.astype(jnp.float32), weights, precision=lax.Precision.HIGHEST)
    magnitude = jnp.sqrt(lax.optimization_barrier(jnp.sum(embedded * embedded, axis=1, keepdims=True)) + epsilon)
    return (embedded / magnitude, magnitude)

def pick_rows(table, index):
    return table[index]

def owner_sum(grads, index):
    return jax.ops.segment_sum(grads.reshape(SHARDS * CAP, PROJ), index.reshape(-1), num_segments=ROWS)

def place_adjoint_total(grads, index):
    return jax.ops.segment_sum(grads.reshape(ROWS * NEG, PROJ), index.reshape(-1), num_segments=SHARDS * CAP)

def reference(hidden, head, pos_local, requests, neg_slot):
    unit_q, magnitude_q = project(hidden[0], head[0])
    unit_p, magnitude_p = project(hidden[1], head[1])
    query_b = unit_q.astype(jnp.bfloat16).reshape(SHARDS, ROWS, PROJ)
    passage_b = unit_p.astype(jnp.bfloat16).reshape(SHARDS, ROWS, PROJ)
    owner_index = jnp.arange(SHARDS, dtype=jnp.int32)[None, :, None]
    pulled = passage_b[owner_index, requests].reshape(SHARDS, SHARDS * CAP, PROJ)
    distractor_places = neg_slot.reshape(SHARDS, ROWS, NEG)
    mined_rows = jax.vmap(pick_rows)(pulled, distractor_places)
    question_inputs = query_b.astype(jnp.float32)
    document_inputs = passage_b.astype(jnp.float32)
    hardest_distractor_inputs = mined_rows.astype(jnp.float32)
    cobatch_logits = jnp.einsum('zek,zgk->zeg', question_inputs, document_inputs) / logit_divisor
    distractor_logits = jnp.einsum('rhk,rhmk->rhm', question_inputs, hardest_distractor_inputs) / logit_divisor
    logits = jnp.concatenate([cobatch_logits, distractor_logits], axis=2)
    softmax_rows = jax.nn.softmax(logits, axis=2)
    target = jax.nn.one_hot(pos_local.reshape(SHARDS, ROWS), ROWS + NEG, dtype=jnp.float32)
    dlog_b = (softmax_rows - target).astype(jnp.bfloat16)
    dlog = lax.optimization_barrier(dlog_b).astype(jnp.float32)
    cobatch_logit_adjoint = dlog[:, :, :ROWS]
    distractor_logit_adjoint = dlog[:, :, ROWS:]
    question_embedding_adjoint = (jnp.einsum('yoq,yqb->yob', cobatch_logit_adjoint, document_inputs) + jnp.einsum('dmp,dmph->dmh', distractor_logit_adjoint, hardest_distractor_inputs)) / logit_divisor
    document_embedding_adjoint = jnp.einsum('cjp,cji->cpi', cobatch_logit_adjoint, question_inputs) / logit_divisor
    update_parameters = distractor_logit_adjoint[:, :, :, None] * question_inputs[:, :, None, :]
    place_adjoint_lines = jax.vmap(place_adjoint_total)(update_parameters, distractor_places) / logit_divisor
    by_owner = place_adjoint_lines.reshape(SHARDS, SHARDS, CAP, PROJ).transpose(1, 0, 2, 3)
    requests_owner = requests.transpose(1, 0, 2)
    added = jax.vmap(owner_sum)(by_owner, requests_owner)
    d_passage = (document_embedding_adjoint + added).reshape(ROWS_ALL, PROJ)
    question_embedding_adjoint = question_embedding_adjoint.reshape(ROWS_ALL, PROJ)
    d_emb_q = (question_embedding_adjoint - unit_q * lax.optimization_barrier(jnp.sum(unit_q * question_embedding_adjoint, axis=1, keepdims=True))) / magnitude_q
    d_emb_p = (d_passage - unit_p * lax.optimization_barrier(jnp.sum(unit_p * d_passage, axis=1, keepdims=True))) / magnitude_p
    grad_q = jnp.einsum('rd,rp->dp', hidden[0].astype(jnp.float32), d_emb_q, precision=lax.Precision.HIGHEST)
    grad_p = jnp.einsum('rd,rp->dp', hidden[1].astype(jnp.float32), d_emb_p, precision=lax.Precision.HIGHEST)
    return jnp.stack([grad_q, grad_p], axis=0)
```

```python
import functools

import jax
import jax.numpy as jnp
from jax import lax
from jax.experimental import pallas as pl
from jax.experimental.pallas import tpu as pltpu
from jax.sharding import PartitionSpec as P

logit_divisor = 0.05
logit_shift = 20.0
epsilon = 1e-06
code_steps = 128.0
code_range = 32700.0
least_value = 1e-30
MESH = pl.DeviceIdType.MESH
VMEM = pltpu.VMEM


def passed_along(block, axis, distance):
    devices = range(lax.axis_size(axis))
    route = [(i - distance, i) for i in devices if i - distance in devices]
    return lax.ppermute(block, axis, route)


def bit_orders(bits):
    low = list(range(bits))
    if bits < 2:
        return [low] * 4
    first = low
    second = [1, 0] + low[2:]
    return [first, second, first, second]


def reduce_kernel(count, orders, hidden_ref, d_ref, out_ref, *scratch):
    bits = len(orders[0])
    parts = len(orders)
    half = count // 2
    rows, depth = hidden_ref.shape
    width = depth // count
    part = d_ref.shape[1] // parts
    terms, acc, codes = scratch[:3]
    sends = scratch[3 : 3 + bits]
    recvs = scratch[3 + bits : 3 + 2 * bits]
    send_sem, recv_sem = scratch[3 + 2 * bits :]
    tower = lax.axis_index("tower")
    me = lax.axis_index("shard")

    def bit_of(number, b):
        return (number // (1 << b)) % 2

    def partner(b):
        return me + (1 - 2 * bit_of(me, b)) * (1 << b)

    barrier = pltpu.get_barrier_semaphore()
    for b in range(bits):
        pl.semaphore_signal(barrier, inc=1, device_id=(tower, partner(b)), device_id_type=MESH)

    for p in range(parts):
        piece = d_ref[:, p * part : (p + 1) * part].T
        upper = piece.astype(jnp.bfloat16)
        terms[p, :part, :] = upper
        terms[p, part:, :] = (piece - upper.astype(jnp.float32)).astype(jnp.bfloat16)

    def product(p, m, leading):
        order = orders[p]
        block = 0
        for t, b in enumerate(order):
            if t == 0:
                own = (bit_of(me, b) + leading) % 2
            else:
                own = (bit_of(me, b) + bit_of(m, bits - 1 - t)) % 2
            block = block + own * (1 << b)
        columns = pl.ds(pl.multiple_of(block * width, width), width)
        both = jnp.dot(terms[p], hidden_ref[:, columns], preferred_element_type=jnp.float32)
        return both[:part] + both[part:]

    def encode(buffer, p, m, value):
        largest = jnp.maximum(jnp.max(jnp.abs(value), axis=0, keepdims=True), least_value)
        code = jnp.ceil(jnp.log2(largest) * code_steps)
        scaled = value * (jnp.exp2(code * (-1.0 / code_steps)) * code_range)
        whole = jnp.round(scaled).astype(jnp.int32).astype(jnp.int16)
        buffer[p, pl.ds(pl.multiple_of(m * part, part), part), :] = whole
        codes[pl.ds(m, 1), :] = code

    def finish(buffer, p, blocks):
        buffer[p, blocks * part : blocks * part + 16, :] = (
            codes[...].astype(jnp.int32).astype(jnp.int16)
        )

    def copy_of(p, k):
        return pltpu.make_async_remote_copy(
            src_ref=sends[k].at[p],
            dst_ref=recvs[k].at[p],
            send_sem=send_sem.at[p, k],
            recv_sem=recv_sem.at[p, k],
            device_id=(tower, partner(orders[p][k])),
            device_id_type=MESH,
        )

    codes[...] = jnp.zeros_like(codes)
    for p in range(parts):

        def first_half(m, carry):
            encode(sends[0], p, m, product(p, m, 1))
            return carry

        lax.fori_loop(0, half, first_half, 0, unroll=2)
        finish(sends[0], p, half)
        if p == 0:
            pl.semaphore_wait(barrier, bits)
        copy_of(p, 0).start()
    for p in range(parts):

        def second_half(m, carry):
            acc[p, m] = product(p, m, 0)
            return carry

        lax.fori_loop(0, half, second_half, 0, unroll=2)

    for k in range(bits):
        blocks = count >> (k + 1)
        for p in range(parts):
            copy_of(p, k).wait_recv()
            got = recvs[k]
            scales = jnp.exp2(
                got[p, blocks * part : blocks * part + 16, :].astype(jnp.int32).astype(jnp.float32)
                * (1.0 / code_steps)
            ) * (1.0 / code_range)
            codes[...] = scales

            def summed(m):
                coded = got[p, pl.ds(pl.multiple_of(m * part, part), part), :]
                value = coded.astype(jnp.int32).astype(jnp.float32)
                return acc[p, m] + value * codes[pl.ds(m, 1), :]

            if k + 1 < bits:
                left = blocks // 2

                def onward(m, carry):
                    acc[p, left + m] = summed(left + m)
                    return carry

                lax.fori_loop(0, left, onward, 0)

                def kept(m, carry):
                    acc[p, m] = summed(m)
                    return carry

                lax.fori_loop(0, left, kept, 0)
                codes[...] = jnp.zeros_like(codes)

                def coded_again(m, carry):
                    encode(sends[k + 1], p, m, acc[p, left + m])
                    return carry

                lax.fori_loop(0, left, coded_again, 0)
                finish(sends[k + 1], p, left)
                copy_of(p, k + 1).start()
            else:
                out_ref[:, p * part : (p + 1) * part] = summed(0).T
    for k in range(bits):
        for p in range(parts):
            copy_of(p, k).wait_send()


def reduced_product(count, hidden_rows, d_embedded):
    rows, depth = hidden_rows.shape
    columns = d_embedded.shape[1]
    bits = count.bit_length() - 1
    orders = bit_orders(bits)
    parts = len(orders)
    part, width = columns // parts, depth // count
    buffers = [
        VMEM((parts, (count >> (k + 1)) * part + 16, width), jnp.int16) for k in range(bits)
    ]
    return pl.pallas_call(
        functools.partial(reduce_kernel, count, orders),
        out_shape=jax.ShapeDtypeStruct((width, columns), jnp.float32),
        in_specs=[pl.BlockSpec(memory_space=VMEM)] * 2,
        out_specs=pl.BlockSpec(memory_space=VMEM),
        scratch_shapes=[
            VMEM((parts, 2 * part, rows), jnp.bfloat16),
            VMEM((parts, count // 2, part, width), jnp.float32),
            VMEM((16, width), jnp.float32),
        ]
        + buffers
        + buffers
        + [pltpu.SemaphoreType.DMA((parts, bits)), pltpu.SemaphoreType.DMA((parts, bits))],
        compiler_params=pltpu.CompilerParams(
            collective_id=0, has_side_effects=True, vmem_limit_bytes=40 * 1024 * 1024
        ),
        cost_estimate=pl.CostEstimate(
            flops=4 * rows * depth * columns, bytes_accessed=8 * rows * depth, transcendentals=0
        ),
    )(hidden_rows, d_embedded)


def shards(hidden, head, pos_local, requests, neg_slot):
    hidden_rows = hidden[0]
    weights = head[0]
    row_count, depth = hidden_rows.shape
    shard_count = lax.axis_size("shard")
    slot_count = requests.shape[2]
    neg_count = neg_slot.shape[1]
    slot_total = shard_count * slot_count
    embedded = jnp.dot(
        hidden_rows, weights, precision=lax.Precision.HIGHEST, preferred_element_type=jnp.float32
    )
    magnitude = jnp.sqrt(jnp.sum(embedded * embedded, axis=1, keepdims=True) + epsilon)
    unit_rows = embedded / magnitude
    normalized = unit_rows.astype(jnp.bfloat16)
    wanted_rows = requests[:, 0, :]
    flat_wanted = wanted_rows.reshape(-1)
    row_ids = jnp.arange(row_count, dtype=jnp.int32)
    owner_table = (row_ids[:, None] == flat_wanted[None, :]).astype(jnp.bfloat16)
    picked = lax.dot_general(
        owner_table, normalized, (((0,), (0,)), ((), ())), preferred_element_type=jnp.float32
    ).astype(jnp.bfloat16)
    sent_rows = lax.all_to_all(
        picked.reshape(shard_count, slot_count, -1),
        "shard",
        split_axis=0,
        concat_axis=0,
        tiled=True,
    )
    joined_rows = jnp.concatenate([normalized, sent_rows.reshape(slot_total, -1)], axis=0)
    arrived_rows = passed_along(joined_rows, "tower", -1)
    scores = jnp.exp(
        jnp.einsum("ot,bt->ob", normalized, arrived_rows, preferred_element_type=jnp.float32)
        / logit_divisor
        - logit_shift
    )
    slot_ids = jnp.arange(slot_total, dtype=jnp.int32)[None, :]
    slot_uses = jnp.zeros((row_count, slot_total), jnp.float32)
    for column in range(neg_count):
        slot_uses = slot_uses + (neg_slot[:, column : column + 1] == slot_ids).astype(jnp.float32)
    cobatch, mined = scores[:, :row_count], scores[:, row_count:]
    total = jnp.sum(cobatch, axis=1, keepdims=True) + jnp.sum(
        mined * slot_uses, axis=1, keepdims=True
    )
    target = (pos_local[:, None] == row_ids[None, :]).astype(jnp.float32)
    dlog = (cobatch / total - target).astype(jnp.bfloat16)
    slot_weight = slot_uses * lax.reduce_precision(mined / total, 8, 7)
    query_grad = (
        jnp.dot(dlog, arrived_rows[:row_count], preferred_element_type=jnp.float32)
        + jnp.dot(
            slot_weight,
            arrived_rows[row_count:].astype(jnp.float32),
            precision=lax.Precision.HIGHEST,
        )
    ) / logit_divisor
    passage_grad = (
        jnp.einsum("en,er->nr", dlog, normalized, preferred_element_type=jnp.float32)
        / logit_divisor
    )
    slot_grad = (
        jnp.dot(slot_weight.T, normalized.astype(jnp.float32), precision=lax.Precision.HIGHEST)
        / logit_divisor
    )
    joined_grads = jnp.concatenate([passage_grad, slot_grad], axis=0)
    arrived_grads = passed_along(joined_grads, "tower", 1)
    got_inbatch = arrived_grads[:row_count]
    got_slots = arrived_grads[row_count:].reshape(shard_count, slot_count, -1)
    returned_slots = lax.all_to_all(
        got_slots.astype(jnp.bfloat16), "shard", split_axis=0, concat_axis=0, tiled=True
    )
    returned = got_inbatch + jnp.dot(
        owner_table, returned_slots.reshape(slot_total, -1), preferred_element_type=jnp.float32
    )
    is_query = lax.axis_index("tower") == 0
    d_unit = jnp.where(is_query, query_grad, returned)
    d_embedded = (
        d_unit - unit_rows * jnp.sum(unit_rows * d_unit, axis=1, keepdims=True)
    ) / magnitude
    power_of_two = shard_count & (shard_count - 1) == 0 and shard_count > 1
    if power_of_two and (depth // shard_count) % 128 == 0:
        return reduced_product(shard_count, hidden_rows, d_embedded)[None]
    head_grad = lax.psum_scatter(
        jnp.einsum(
            "rd,rp->dp",
            hidden_rows,
            d_embedded,
            precision=lax.Precision.HIGHEST,
            preferred_element_type=jnp.float32,
        ),
        "shard",
        scatter_dimension=0,
        tiled=True,
    )
    return head_grad[None]


def solution(mesh):
    placed = (
        P("tower", "shard", None),
        P("tower", None, None),
        P("shard"),
        P(None, "shard", None),
        P("shard", None),
    )
    return jax.shard_map(
        shards, mesh=mesh, in_specs=placed, out_specs=P("tower", "shard", None), check_vma=False
    )
```

```python
import functools

import jax
import jax.numpy as jnp
from jax import lax
from jax.experimental import pallas as pl
from jax.experimental.pallas import tpu as pltpu
from jax.sharding import PartitionSpec as P

logit_divisor = 0.05
logit_shift = 20.0
epsilon = 1e-06
code_steps = 128.0
code_range = 32700.0
least_value = 1e-30
MESH = pl.DeviceIdType.MESH
VMEM = pltpu.VMEM


def passed_along(block, axis, distance):
    devices = range(lax.axis_size(axis))
    route = [(i - distance, i) for i in devices if i - distance in devices]
    return lax.ppermute(block, axis, route)


def bit_orders(bits):
    low = list(range(bits))
    if bits < 2:
        return [low] * 4
    first = low
    second = [1, 0] + low[2:]
    return [first, second, first, second]


def front(
    count,
    hidden_hbm,
    head_hbm,
    positive_ref,
    wanted_ref,
    negative_ref,
    hidden_ref,
    head_ref,
    unit_ref,
    scale_ref,
    unit_b_ref,
    mate_ref,
    dlog_ref,
    dlog_got_ref,
    grad_ref,
    slots_out_ref,
    slots_in_ref,
    load_sem,
    pair_sem,
    slot_send_sem,
    slot_recv_sem,
    greet,
):
    tower = lax.axis_index("tower")
    me = lax.axis_index("shard")
    rows, depth = hidden_ref.shape
    columns = unit_ref.shape[1]
    chunks = load_sem.shape[1]
    chunk = depth // chunks
    slots = count * slots_in_ref.shape[1]
    lane_groups = columns // 128
    picks = slots // (count * lane_groups)
    per_owner = picks * lane_groups

    def loads(c):
        span = pl.ds(c * chunk, chunk)
        return (
            pltpu.make_async_copy(hidden_hbm.at[:, span], hidden_ref.at[:, span], load_sem.at[0, c]),
            pltpu.make_async_copy(head_hbm.at[span, :], head_ref.at[span, :], load_sem.at[1, c]),
        )

    def to_mate(source, target, which):
        return pltpu.make_async_remote_copy(
            src_ref=source,
            dst_ref=target,
            send_sem=pair_sem.at[which],
            recv_sem=pair_sem.at[which + 1],
            device_id=(1 - tower, me),
            device_id_type=MESH,
        )

    def slot_copy(i):
        other = lax.rem(me + i, count)
        return pltpu.make_async_remote_copy(
            src_ref=slots_out_ref.at[other],
            dst_ref=slots_in_ref.at[me],
            send_sem=slot_send_sem.at[i],
            recv_sem=slot_recv_sem.at[me],
            device_id=(1 - tower, other),
            device_id_type=MESH,
        )

    def slots_arrive():
        for o in range(count):
            pltpu.make_async_remote_copy(
                src_ref=slots_out_ref.at[o],
                dst_ref=slots_in_ref.at[o],
                send_sem=slot_send_sem.at[o],
                recv_sem=slot_recv_sem.at[o],
                device_id=(1 - tower, me),
                device_id_type=MESH,
            ).wait_recv()

    def dot(left, right, dims):
        return lax.dot_general(left, right, (dims, ((), ())), preferred_element_type=jnp.float32)

    def group_of(shape, axis):
        return (lax.broadcasted_iota(jnp.int32, shape, axis) >> (picks.bit_length() - 1)) & (
            lane_groups - 1
        )

    def send_slots(table):
        group = group_of((slots, 128), 0)
        packed = jnp.zeros((slots, 128), jnp.float32)
        for q in range(lane_groups):
            packed = packed + jnp.where(group == q, table[:, q * 128 : (q + 1) * 128], 0.0)
        packed = packed.astype(jnp.bfloat16)
        for o in range(count):
            slots_out_ref[o] = packed[o * per_owner : (o + 1) * per_owner, :]
        for i in range(count):
            slot_copy(i).start()

    def read_slots():
        packed = jnp.concatenate([slots_in_ref[o] for o in range(count)], axis=0)
        row = lax.broadcasted_iota(jnp.int32, (slots, slots), 0)
        column = lax.broadcasted_iota(jnp.int32, (slots, slots), 1)
        low, high = picks - 1, -per_owner
        same = ((row & low) == (column & low)) & ((row & high) == (column & high))
        group = group_of((slots, slots), 1)
        pieces = []
        for q in range(lane_groups):
            chosen = (same & (group == q)).astype(jnp.float32).astype(jnp.bfloat16)
            pieces.append(dot(chosen, packed, ((1,), (0,))).astype(jnp.bfloat16))
        return jnp.concatenate(pieces, axis=1)

    for c in range(chunks):
        for load in loads(c):
            load.start()
    for c in range(chunks):
        for load in loads(c):
            load.wait()
        span = slice(c * chunk, (c + 1) * chunk)
        weights = head_ref[span, :]
        first = weights.astype(jnp.bfloat16)
        left = weights - first.astype(jnp.float32)
        second = left.astype(jnp.bfloat16)
        third = (left - second.astype(jnp.float32)).astype(jnp.bfloat16)
        block = hidden_ref[:, span]
        term = (
            dot(block, third, ((1,), (0,)))
            + dot(block, second, ((1,), (0,)))
            + dot(block, first, ((1,), (0,)))
        )
        if c == 0:
            unit_ref[...] = term
        else:
            unit_ref[...] += term
    embedded = unit_ref[...]
    inverse = 1.0 / jnp.sqrt(jnp.sum(embedded * embedded, axis=1, keepdims=True) + epsilon)
    unit = embedded * inverse
    unit_ref[...] = unit
    scale_ref[...] = inverse
    unit_b_ref[...] = unit.astype(jnp.bfloat16)
    greet()
    to_mate(unit_b_ref, mate_ref, 0).start()
    lane_owner = lax.broadcasted_iota(jnp.int32, (rows, slots), 0) == wanted_ref[...]

    @pl.when(tower == 1)
    def _():
        table = lane_owner.astype(jnp.float32).astype(jnp.bfloat16)
        send_slots(dot(table, unit_b_ref[...], ((0,), (0,))))
        to_mate(unit_b_ref, mate_ref, 0).wait_recv()
        to_mate(dlog_ref, dlog_got_ref, 2).wait_recv()
        grad_ref[...] = dot(dlog_got_ref[...], mate_ref[...], ((0,), (0,))) / logit_divisor
        slots_arrive()
        once = lane_owner & (group_of((rows, slots), 1) == 0)
        grad_ref[...] += dot(
            once.astype(jnp.float32).astype(jnp.bfloat16), read_slots(), ((1,), (0,))
        )

    @pl.when(tower == 0)
    def _():
        lane = lax.broadcasted_iota(jnp.int32, (rows, slots), 1)
        slot_id = (lane >> (per_owner.bit_length() - 1)) * picks + (lane & (picks - 1))
        uses = jnp.zeros((rows, slots), jnp.float32)
        for k in range(negative_ref.shape[1]):
            uses = uses + (negative_ref[:, k : k + 1] == slot_id).astype(jnp.float32)
        once = (group_of((rows, slots), 1) == 0).astype(jnp.float32)
        to_mate(unit_b_ref, mate_ref, 0).wait_recv()
        cobatch = jnp.exp(
            dot(unit_b_ref[...], mate_ref[...], ((1,), (1,))) / logit_divisor - logit_shift
        )
        cobatch_sum = jnp.sum(cobatch, axis=1, keepdims=True)
        slots_arrive()
        pulled = read_slots()
        mined = jnp.exp(
            dot(unit_b_ref[...], pulled, ((1,), (1,))) / logit_divisor - logit_shift
        )
        share = 1.0 / (cobatch_sum + jnp.sum(mined * uses * once, axis=1, keepdims=True))
        target = lax.broadcasted_iota(jnp.int32, (rows, rows), 1) == positive_ref[...]
        dlog_ref[...] = (cobatch * share - target.astype(jnp.float32)).astype(jnp.bfloat16)
        to_mate(dlog_ref, dlog_got_ref, 2).start()
        weight = uses * (mined * share).astype(jnp.bfloat16).astype(jnp.float32)
        upper = weight.astype(jnp.bfloat16)
        lower = (weight - upper.astype(jnp.float32)).astype(jnp.bfloat16)
        slot_grad = dot(upper, unit_b_ref[...], ((0,), (0,))) + dot(
            lower, unit_b_ref[...], ((0,), (0,))
        )
        send_slots(slot_grad / logit_divisor)
        once_b = once.astype(jnp.bfloat16)
        grad_ref[...] = (
            dot(dlog_ref[...], mate_ref[...], ((1,), (0,)))
            + dot(upper * once_b, pulled, ((1,), (0,)))
            + dot(lower * once_b, pulled, ((1,), (0,)))
        ) / logit_divisor
        to_mate(dlog_ref, dlog_got_ref, 2).wait_send()

    d_unit, unit = grad_ref[...], unit_ref[...]
    along = jnp.sum(unit * d_unit, axis=1, keepdims=True)
    grad_ref[...] = (d_unit - unit * along) * scale_ref[...]
    to_mate(unit_b_ref, mate_ref, 0).wait_send()
    for i in range(count):
        slot_copy(i).wait_send()


def whole_kernel(
    count, orders, hidden_hbm, head_hbm, positive_ref, wanted_ref, negative_ref, out_ref, *scratch
):
    bits = len(orders[0])
    parts = len(orders)
    half = count // 2
    hidden_ref, grad_ref = scratch[0], scratch[8]
    front_refs, scratch = scratch[:15], scratch[15:]
    d_ref = grad_ref
    rows, depth = hidden_ref.shape
    width = depth // count
    part = d_ref.shape[1] // parts
    terms, acc, codes = scratch[:3]
    sends = scratch[3 : 3 + bits]
    recvs = scratch[3 + bits : 3 + 2 * bits]
    send_sem, recv_sem = scratch[3 + 2 * bits :]
    tower = lax.axis_index("tower")
    me = lax.axis_index("shard")

    def bit_of(number, b):
        return (number // (1 << b)) % 2

    def partner(b):
        return me + (1 - 2 * bit_of(me, b)) * (1 << b)

    barrier = pltpu.get_barrier_semaphore()
    for b in range(bits):
        pl.semaphore_signal(barrier, inc=1, device_id=(tower, partner(b)), device_id_type=MESH)
    for o in range(count):
        pl.semaphore_signal(barrier, inc=1, device_id=(1 - tower, o), device_id_type=MESH)

    def greet():
        pl.semaphore_wait(barrier, bits + count)

    front(count, hidden_hbm, head_hbm, positive_ref, wanted_ref, negative_ref, *front_refs, greet)
    for p in range(parts):
        piece = d_ref[:, p * part : (p + 1) * part].T
        upper = piece.astype(jnp.bfloat16)
        terms[p, :part, :] = upper
        terms[p, part:, :] = (piece - upper.astype(jnp.float32)).astype(jnp.bfloat16)

    def product(p, m, leading):
        order = orders[p]
        block = 0
        for t, b in enumerate(order):
            if t == 0:
                own = (bit_of(me, b) + leading) % 2
            else:
                own = (bit_of(me, b) + bit_of(m, bits - 1 - t)) % 2
            block = block + own * (1 << b)
        columns = pl.ds(pl.multiple_of(block * width, width), width)
        both = jnp.dot(terms[p], hidden_ref[:, columns], preferred_element_type=jnp.float32)
        return both[:part] + both[part:]

    def encode(buffer, p, m, value):
        largest = jnp.maximum(jnp.max(jnp.abs(value), axis=0, keepdims=True), least_value)
        code = jnp.ceil(jnp.log2(largest) * code_steps)
        scaled = value * (jnp.exp2(code * (-1.0 / code_steps)) * code_range)
        whole = jnp.round(scaled).astype(jnp.int32).astype(jnp.int16)
        buffer[p, pl.ds(pl.multiple_of(m * part, part), part), :] = whole
        codes[pl.ds(m, 1), :] = code

    def finish(buffer, p, blocks):
        buffer[p, blocks * part : blocks * part + 16, :] = (
            codes[...].astype(jnp.int32).astype(jnp.int16)
        )

    def copy_of(p, k):
        return pltpu.make_async_remote_copy(
            src_ref=sends[k].at[p],
            dst_ref=recvs[k].at[p],
            send_sem=send_sem.at[p, k],
            recv_sem=recv_sem.at[p, k],
            device_id=(tower, partner(orders[p][k])),
            device_id_type=MESH,
        )

    codes[...] = jnp.zeros_like(codes)
    for p in range(parts):

        def first_half(m, carry):
            encode(sends[0], p, m, product(p, m, 1))
            return carry

        lax.fori_loop(0, half, first_half, 0, unroll=2)
        finish(sends[0], p, half)
        copy_of(p, 0).start()
    for p in range(parts):

        def second_half(m, carry):
            acc[p, m] = product(p, m, 0)
            return carry

        lax.fori_loop(0, half, second_half, 0, unroll=2)

    for k in range(bits):
        blocks = count >> (k + 1)
        for p in range(parts):
            copy_of(p, k).wait_recv()
            got = recvs[k]
            scales = jnp.exp2(
                got[p, blocks * part : blocks * part + 16, :].astype(jnp.int32).astype(jnp.float32)
                * (1.0 / code_steps)
            ) * (1.0 / code_range)
            codes[...] = scales

            def summed(m):
                coded = got[p, pl.ds(pl.multiple_of(m * part, part), part), :]
                value = coded.astype(jnp.int32).astype(jnp.float32)
                return acc[p, m] + value * codes[pl.ds(m, 1), :]

            if k + 1 < bits:
                left = blocks // 2

                def onward(m, carry):
                    acc[p, left + m] = summed(left + m)
                    return carry

                lax.fori_loop(0, left, onward, 0)

                def kept(m, carry):
                    acc[p, m] = summed(m)
                    return carry

                lax.fori_loop(0, left, kept, 0)
                codes[...] = jnp.zeros_like(codes)

                def coded_again(m, carry):
                    encode(sends[k + 1], p, m, acc[p, left + m])
                    return carry

                lax.fori_loop(0, left, coded_again, 0)
                finish(sends[k + 1], p, left)
                copy_of(p, k + 1).start()
            else:
                out_ref[:, p * part : (p + 1) * part] = summed(0).T
    for k in range(bits):
        for p in range(parts):
            copy_of(p, k).wait_send()


def whole_gradient(count, hidden_rows, weights, positive, wanted, negative):
    rows, depth = hidden_rows.shape
    columns = weights.shape[1]
    slots = wanted.shape[1]
    bits = count.bit_length() - 1
    orders = bit_orders(bits)
    parts = len(orders)
    chunks = 8
    part, width = columns // parts, depth // count
    buffers = [
        VMEM((parts, (count >> (k + 1)) * part + 16, width), jnp.int16) for k in range(bits)
    ]
    slot_buffer = VMEM((count, slots // count, 128), jnp.bfloat16)
    return pl.pallas_call(
        functools.partial(whole_kernel, count, orders),
        out_shape=jax.ShapeDtypeStruct((width, columns), jnp.float32),
        in_specs=[pl.BlockSpec(memory_space=pl.ANY)] * 2 + [pl.BlockSpec(memory_space=VMEM)] * 3,
        out_specs=pl.BlockSpec(memory_space=VMEM),
        scratch_shapes=[
            VMEM((rows, depth), jnp.bfloat16),
            VMEM((depth, columns), jnp.float32),
            VMEM((rows, columns), jnp.float32),
            VMEM((rows, 1), jnp.float32),
            VMEM((rows, columns), jnp.bfloat16),
            VMEM((rows, columns), jnp.bfloat16),
            VMEM((rows, rows), jnp.bfloat16),
            VMEM((rows, rows), jnp.bfloat16),
            VMEM((rows, columns), jnp.float32),
            slot_buffer,
            slot_buffer,
            pltpu.SemaphoreType.DMA((2, chunks)),
            pltpu.SemaphoreType.DMA((4,)),
            pltpu.SemaphoreType.DMA((count,)),
            pltpu.SemaphoreType.DMA((count,)),
            VMEM((parts, 2 * part, rows), jnp.bfloat16),
            VMEM((parts, count // 2, part, width), jnp.float32),
            VMEM((16, width), jnp.float32),
        ]
        + buffers
        + buffers
        + [pltpu.SemaphoreType.DMA((parts, bits)), pltpu.SemaphoreType.DMA((parts, bits))],
        compiler_params=pltpu.CompilerParams(
            collective_id=0, has_side_effects=True, vmem_limit_bytes=54 * 1024 * 1024
        ),
        cost_estimate=pl.CostEstimate(
            flops=10 * rows * depth * columns, bytes_accessed=12 * rows * depth, transcendentals=0
        ),
    )(hidden_rows, weights, positive, wanted, negative)


def shards(hidden, head, pos_local, requests, neg_slot):
    hidden_rows = hidden[0]
    weights = head[0]
    row_count, depth = hidden_rows.shape
    shard_count = lax.axis_size("shard")
    slot_count = requests.shape[2]
    neg_count = neg_slot.shape[1]
    slot_total = shard_count * slot_count
    power_of_two = shard_count & (shard_count - 1) == 0 and shard_count > 1
    lane_groups = weights.shape[1] // 128
    if power_of_two and (depth // shard_count) % 128 == 0 and slot_count * lane_groups == 16:
        wanted = jnp.broadcast_to(requests, (shard_count, lane_groups, slot_count))
        return whole_gradient(
            shard_count, hidden_rows, weights, pos_local[:, None], wanted.reshape(1, -1), neg_slot
        )[None]
    embedded = jnp.dot(
        hidden_rows, weights, precision=lax.Precision.HIGHEST, preferred_element_type=jnp.float32
    )
    magnitude = jnp.sqrt(jnp.sum(embedded * embedded, axis=1, keepdims=True) + epsilon)
    unit_rows = embedded / magnitude
    normalized = unit_rows.astype(jnp.bfloat16)
    wanted_rows = requests[:, 0, :]
    flat_wanted = wanted_rows.reshape(-1)
    row_ids = jnp.arange(row_count, dtype=jnp.int32)
    owner_table = (row_ids[:, None] == flat_wanted[None, :]).astype(jnp.bfloat16)
    picked = lax.dot_general(
        owner_table, normalized, (((0,), (0,)), ((), ())), preferred_element_type=jnp.float32
    ).astype(jnp.bfloat16)
    sent_rows = lax.all_to_all(
        picked.reshape(shard_count, slot_count, -1),
        "shard",
        split_axis=0,
        concat_axis=0,
        tiled=True,
    )
    joined_rows = jnp.concatenate([normalized, sent_rows.reshape(slot_total, -1)], axis=0)
    arrived_rows = passed_along(joined_rows, "tower", -1)
    scores = jnp.exp(
        jnp.einsum("ot,bt->ob", normalized, arrived_rows, preferred_element_type=jnp.float32)
        / logit_divisor
        - logit_shift
    )
    slot_ids = jnp.arange(slot_total, dtype=jnp.int32)[None, :]
    slot_uses = jnp.zeros((row_count, slot_total), jnp.float32)
    for column in range(neg_count):
        slot_uses = slot_uses + (neg_slot[:, column : column + 1] == slot_ids).astype(jnp.float32)
    cobatch, mined = scores[:, :row_count], scores[:, row_count:]
    total = jnp.sum(cobatch, axis=1, keepdims=True) + jnp.sum(
        mined * slot_uses, axis=1, keepdims=True
    )
    target = (pos_local[:, None] == row_ids[None, :]).astype(jnp.float32)
    dlog = (cobatch / total - target).astype(jnp.bfloat16)
    slot_weight = slot_uses * lax.reduce_precision(mined / total, 8, 7)
    query_grad = (
        jnp.dot(dlog, arrived_rows[:row_count], preferred_element_type=jnp.float32)
        + jnp.dot(
            slot_weight,
            arrived_rows[row_count:].astype(jnp.float32),
            precision=lax.Precision.HIGHEST,
        )
    ) / logit_divisor
    passage_grad = (
        jnp.einsum("en,er->nr", dlog, normalized, preferred_element_type=jnp.float32)
        / logit_divisor
    )
    slot_grad = (
        jnp.dot(slot_weight.T, normalized.astype(jnp.float32), precision=lax.Precision.HIGHEST)
        / logit_divisor
    )
    joined_grads = jnp.concatenate([passage_grad, slot_grad], axis=0)
    arrived_grads = passed_along(joined_grads, "tower", 1)
    got_inbatch = arrived_grads[:row_count]
    got_slots = arrived_grads[row_count:].reshape(shard_count, slot_count, -1)
    returned_slots = lax.all_to_all(
        got_slots.astype(jnp.bfloat16), "shard", split_axis=0, concat_axis=0, tiled=True
    )
    returned = got_inbatch + jnp.dot(
        owner_table, returned_slots.reshape(slot_total, -1), preferred_element_type=jnp.float32
    )
    is_query = lax.axis_index("tower") == 0
    d_unit = jnp.where(is_query, query_grad, returned)
    d_embedded = (
        d_unit - unit_rows * jnp.sum(unit_rows * d_unit, axis=1, keepdims=True)
    ) / magnitude
    head_grad = lax.psum_scatter(
        jnp.einsum(
            "rd,rp->dp",
            hidden_rows,
            d_embedded,
            precision=lax.Precision.HIGHEST,
            preferred_element_type=jnp.float32,
        ),
        "shard",
        scatter_dimension=0,
        tiled=True,
    )
    return head_grad[None]


def solution(mesh):
    placed = (
        P("tower", "shard", None),
        P("tower", None, None),
        P("shard"),
        P(None, "shard", None),
        P("shard", None),
    )
    return jax.shard_map(
        shards, mesh=mesh, in_specs=placed, out_specs=P("tower", "shard", None), check_vma=False
    )
```

```python
import functools

import jax
import jax.numpy as jnp
from jax import lax
from jax.experimental import pallas as pl
from jax.experimental.pallas import tpu as pltpu
from jax.sharding import PartitionSpec as P

logit_divisor = 0.05
logit_shift = 20.0
epsilon = 1e-06
code_steps = 128.0
code_range = 32700.0
PIECES, STAGGER, UNROLL = 2, False, 2
least_value = 1e-30
MESH = pl.DeviceIdType.MESH
VMEM = pltpu.VMEM


def passed_along(block, axis, distance):
    devices = range(lax.axis_size(axis))
    route = [(i - distance, i) for i in devices if i - distance in devices]
    return lax.ppermute(block, axis, route)


def part_plan(columns, bits):
    low = list(range(bits))
    if bits < 3:
        return [(columns // 2, low)] * 2
    rest = low[3:]
    orders = ([0, 1, 2] + rest, [1, 2, 0] + rest, [2, 0, 1] + rest)
    piece = columns // PIECES
    wide = (piece * 11 // 32 + 15) // 16 * 16
    sizes = [wide, wide, piece - 2 * wide]
    return [(size, order) for _ in range(PIECES) for size, order in zip(sizes, orders)]


def front(
    count,
    hidden_hbm,
    head_hbm,
    positive_ref,
    wanted_ref,
    negative_ref,
    hidden_ref,
    head_ref,
    unit_ref,
    scale_ref,
    unit_b_ref,
    mate_ref,
    dlog_ref,
    dlog_got_ref,
    grad_ref,
    slots_out_ref,
    slots_in_ref,
    load_sem,
    pair_sem,
    slot_send_sem,
    slot_recv_sem,
    greet,
):
    tower = lax.axis_index("tower")
    me = lax.axis_index("shard")
    rows, depth = hidden_ref.shape
    columns = unit_ref.shape[1]
    chunks = load_sem.shape[1]
    chunk = depth // chunks
    slots = count * slots_in_ref.shape[1]
    lane_groups = columns // 128
    picks = slots // (count * lane_groups)
    per_owner = picks * lane_groups

    def loads(c):
        span = pl.ds(c * chunk, chunk)
        return (
            pltpu.make_async_copy(hidden_hbm.at[:, span], hidden_ref.at[:, span], load_sem.at[0, c]),
            pltpu.make_async_copy(head_hbm.at[span, :], head_ref.at[span, :], load_sem.at[1, c]),
        )

    def to_mate(source, target, which):
        return pltpu.make_async_remote_copy(
            src_ref=source,
            dst_ref=target,
            send_sem=pair_sem.at[which],
            recv_sem=pair_sem.at[which + 1],
            device_id=(1 - tower, me),
            device_id_type=MESH,
        )

    def slot_copy(i):
        other = lax.rem(me + i, count)
        return pltpu.make_async_remote_copy(
            src_ref=slots_out_ref.at[other],
            dst_ref=slots_in_ref.at[me],
            send_sem=slot_send_sem.at[i],
            recv_sem=slot_recv_sem.at[me],
            device_id=(1 - tower, other),
            device_id_type=MESH,
        )

    def slots_arrive():
        for o in range(count):
            pltpu.make_async_remote_copy(
                src_ref=slots_out_ref.at[o],
                dst_ref=slots_in_ref.at[o],
                send_sem=slot_send_sem.at[o],
                recv_sem=slot_recv_sem.at[o],
                device_id=(1 - tower, me),
                device_id_type=MESH,
            ).wait_recv()

    def dot(left, right, dims):
        return lax.dot_general(left, right, (dims, ((), ())), preferred_element_type=jnp.float32)

    def group_of(shape, axis):
        return (lax.broadcasted_iota(jnp.int32, shape, axis) >> (picks.bit_length() - 1)) & (
            lane_groups - 1
        )

    def send_slots(table):
        group = group_of((slots, 128), 0)
        packed = jnp.zeros((slots, 128), jnp.float32)
        for q in range(lane_groups):
            packed = packed + jnp.where(group == q, table[:, q * 128 : (q + 1) * 128], 0.0)
        packed = packed.astype(jnp.bfloat16)
        for o in range(count):
            slots_out_ref[o] = packed[o * per_owner : (o + 1) * per_owner, :]
        for i in range(count):
            slot_copy(i).start()

    def read_slots():
        packed = jnp.concatenate([slots_in_ref[o] for o in range(count)], axis=0)
        row = lax.broadcasted_iota(jnp.int32, (slots, slots), 0)
        column = lax.broadcasted_iota(jnp.int32, (slots, slots), 1)
        low, high = picks - 1, -per_owner
        same = ((row & low) == (column & low)) & ((row & high) == (column & high))
        group = group_of((slots, slots), 1)
        pieces = []
        for q in range(lane_groups):
            chosen = (same & (group == q)).astype(jnp.float32).astype(jnp.bfloat16)
            pieces.append(dot(chosen, packed, ((1,), (0,))).astype(jnp.bfloat16))
        return jnp.concatenate(pieces, axis=1)

    for c in range(chunks):
        for load in loads(c):
            load.start()
    for c in range(chunks):
        for load in loads(c):
            load.wait()
        span = slice(c * chunk, (c + 1) * chunk)
        weights = head_ref[span, :]
        first = weights.astype(jnp.bfloat16)
        left = weights - first.astype(jnp.float32)
        second = left.astype(jnp.bfloat16)
        third = (left - second.astype(jnp.float32)).astype(jnp.bfloat16)
        block = hidden_ref[:, span]
        term = (
            dot(block, third, ((1,), (0,)))
            + dot(block, second, ((1,), (0,)))
            + dot(block, first, ((1,), (0,)))
        )
        if c == 0:
            unit_ref[...] = term
        else:
            unit_ref[...] += term
    embedded = unit_ref[...]
    inverse = 1.0 / jnp.sqrt(jnp.sum(embedded * embedded, axis=1, keepdims=True) + epsilon)
    unit = embedded * inverse
    unit_ref[...] = unit
    scale_ref[...] = inverse
    unit_b_ref[...] = unit.astype(jnp.bfloat16)
    greet()
    to_mate(unit_b_ref, mate_ref, 0).start()
    lane_owner = lax.broadcasted_iota(jnp.int32, (rows, slots), 0) == wanted_ref[...]

    @pl.when(tower == 1)
    def _():
        table = lane_owner.astype(jnp.float32).astype(jnp.bfloat16)
        send_slots(dot(table, unit_b_ref[...], ((0,), (0,))))
        to_mate(unit_b_ref, mate_ref, 0).wait_recv()
        to_mate(dlog_ref, dlog_got_ref, 2).wait_recv()
        grad_ref[...] = dot(dlog_got_ref[...], mate_ref[...], ((0,), (0,))) / logit_divisor
        slots_arrive()
        once = lane_owner & (group_of((rows, slots), 1) == 0)
        grad_ref[...] += dot(
            once.astype(jnp.float32).astype(jnp.bfloat16), read_slots(), ((1,), (0,))
        )

    @pl.when(tower == 0)
    def _():
        lane = lax.broadcasted_iota(jnp.int32, (rows, slots), 1)
        slot_id = (lane >> (per_owner.bit_length() - 1)) * picks + (lane & (picks - 1))
        uses = jnp.zeros((rows, slots), jnp.float32)
        for k in range(negative_ref.shape[1]):
            uses = uses + (negative_ref[:, k : k + 1] == slot_id).astype(jnp.float32)
        once = (group_of((rows, slots), 1) == 0).astype(jnp.float32)
        to_mate(unit_b_ref, mate_ref, 0).wait_recv()
        cobatch = jnp.exp(
            dot(unit_b_ref[...], mate_ref[...], ((1,), (1,))) / logit_divisor - logit_shift
        )
        cobatch_sum = jnp.sum(cobatch, axis=1, keepdims=True)
        slots_arrive()
        pulled = read_slots()
        mined = jnp.exp(
            dot(unit_b_ref[...], pulled, ((1,), (1,))) / logit_divisor - logit_shift
        )
        share = 1.0 / (cobatch_sum + jnp.sum(mined * uses * once, axis=1, keepdims=True))
        target = lax.broadcasted_iota(jnp.int32, (rows, rows), 1) == positive_ref[...]
        dlog_ref[...] = (cobatch * share - target.astype(jnp.float32)).astype(jnp.bfloat16)
        to_mate(dlog_ref, dlog_got_ref, 2).start()
        weight = uses * (mined * share).astype(jnp.bfloat16).astype(jnp.float32)
        upper = weight.astype(jnp.bfloat16)
        lower = (weight - upper.astype(jnp.float32)).astype(jnp.bfloat16)
        slot_grad = dot(upper, unit_b_ref[...], ((0,), (0,))) + dot(
            lower, unit_b_ref[...], ((0,), (0,))
        )
        send_slots(slot_grad / logit_divisor)
        once_b = once.astype(jnp.bfloat16)
        grad_ref[...] = (
            dot(dlog_ref[...], mate_ref[...], ((1,), (0,)))
            + dot(upper * once_b, pulled, ((1,), (0,)))
            + dot(lower * once_b, pulled, ((1,), (0,)))
        ) / logit_divisor
        to_mate(dlog_ref, dlog_got_ref, 2).wait_send()

    d_unit, unit = grad_ref[...], unit_ref[...]
    along = jnp.sum(unit * d_unit, axis=1, keepdims=True)
    grad_ref[...] = (d_unit - unit * along) * scale_ref[...]
    to_mate(unit_b_ref, mate_ref, 0).wait_send()
    for i in range(count):
        slot_copy(i).wait_send()


def row_starts(count, plan):
    starts, messages, column, row = [], {}, 0, 0
    for p, (part, order) in enumerate(plan):
        starts.append(column)
        column += part
        for k in range(len(order)):
            messages[p, k] = row
            row += (count >> (k + 1)) * part + 16
    return starts, messages, row


def whole_kernel(
    count, plan, hidden_hbm, head_hbm, positive_ref, wanted_ref, negative_ref, out_ref, *scratch
):
    bits = len(plan[0][1])
    parts = len(plan)
    starts, messages, _ = row_starts(count, plan)
    half = count // 2
    hidden_ref, d_ref = scratch[0], scratch[8]
    front_refs, scratch = scratch[:15], scratch[15:]
    rows, depth = hidden_ref.shape
    width = depth // count
    terms, acc, total, codes, scales, sent, got, send_sem, recv_sem = scratch
    tower = lax.axis_index("tower")
    me = lax.axis_index("shard")

    def bit_of(number, b):
        return (number // (1 << b)) % 2

    def partner(b):
        return me + (1 - 2 * bit_of(me, b)) * (1 << b)

    barrier = pltpu.get_barrier_semaphore()
    for b in range(bits):
        pl.semaphore_signal(barrier, inc=1, device_id=(tower, partner(b)), device_id_type=MESH)
    for o in range(count):
        pl.semaphore_signal(barrier, inc=1, device_id=(1 - tower, o), device_id_type=MESH)

    def greet():
        pl.semaphore_wait(barrier, bits + count)

    front(count, hidden_hbm, head_hbm, positive_ref, wanted_ref, negative_ref, *front_refs, greet)
    turned = d_ref[...].T
    upper = turned.astype(jnp.bfloat16)
    lower = (turned - upper.astype(jnp.float32)).astype(jnp.bfloat16)
    for p, (part, _) in enumerate(plan):
        start = starts[p]
        terms[2 * start : 2 * start + part, :] = upper[start : start + part, :]
        terms[2 * start + part : 2 * (start + part), :] = lower[start : start + part, :]

    def product(p, m, leading):
        part, order = plan[p]
        block = 0
        for t, b in enumerate(order):
            if t == 0:
                own = (bit_of(me, b) + leading) % 2
            else:
                own = (bit_of(me, b) + bit_of(m, bits - 1 - t)) % 2
            block = block + own * (1 << b)
        columns = pl.ds(pl.multiple_of(block * width, width), width)
        both = jnp.dot(
            terms[2 * starts[p] : 2 * (starts[p] + part), :],
            hidden_ref[:, columns],
            preferred_element_type=jnp.float32,
        )
        return both[:part] + both[part:]

    def encode(p, k, m, value):
        part = plan[p][0]
        largest = jnp.maximum(jnp.max(jnp.abs(value), axis=0, keepdims=True), least_value)
        code = jnp.ceil(jnp.log2(largest) * code_steps)
        scaled = value * (jnp.exp2(code * (-1.0 / code_steps)) * code_range)
        whole = jnp.round(scaled).astype(jnp.int32).astype(jnp.int16)
        sent[pl.ds(pl.multiple_of(messages[p, k] + m * part, 16), part), :] = whole
        codes[pl.ds(m, 1), :] = code

    def copy_of(p, k):
        part, order = plan[p]
        span = pl.ds(messages[p, k], (count >> (k + 1)) * part + 16)
        return pltpu.make_async_remote_copy(
            src_ref=sent.at[span, :],
            dst_ref=got.at[span, :],
            send_sem=send_sem.at[p, k],
            recv_sem=recv_sem.at[p, k],
            device_id=(tower, partner(order[k])),
            device_id_type=MESH,
        )

    def finish(p, k):
        end = messages[p, k] + (count >> (k + 1)) * plan[p][0]
        sent[end : end + 16, :] = codes[...].astype(jnp.int32).astype(jnp.int16)

    codes[...] = jnp.zeros_like(codes)
    for p in range(parts):

        def first_half(m, carry):
            encode(p, 0, m, product(p, m, 1))
            return carry

        lax.fori_loop(0, half, first_half, 0, unroll=UNROLL)
        finish(p, 0)
        if not STAGGER or p < parts // PIECES:
            copy_of(p, 0).start()
    for p, (part, _) in enumerate(plan):

        def second_half(m, carry):
            acc[m, starts[p] : starts[p] + part, :] = product(p, m, 0)
            return carry

        lax.fori_loop(0, half, second_half, 0, unroll=UNROLL)
    waited = set()
    if STAGGER:
        for p in range(parts // PIECES, parts):
            copy_of(p - parts // PIECES, 0).wait_send()
            waited.add((p - parts // PIECES, 0))
            copy_of(p, 0).start()

    steps = [(k, p) for k in range(bits) for p in range(parts)]
    if STAGGER:
        lead = parts // PIECES
        steps = sorted(steps, key=lambda step: (step[0] + step[1] // lead, step[1]))
    for k, p in steps:
        part = plan[p][0]
        blocks = count >> (k + 1)
        left = blocks // 2
        own = slice(starts[p], starts[p] + part)
        copy_of(p, k).wait_recv()
        end = messages[p, k] + blocks * part
        scales[...] = jnp.exp2(
            got[end : end + 16, :].astype(jnp.int32).astype(jnp.float32) * (1.0 / code_steps)
        ) * (1.0 / code_range)

        def summed(m):
            coded = got[pl.ds(pl.multiple_of(messages[p, k] + m * part, 16), part), :]
            value = coded.astype(jnp.int32).astype(jnp.float32)
            return acc[m, own, :] + value * scales[pl.ds(m, 1), :]

        if k + 1 < bits:

            def onward(m, carry):
                encode(p, k + 1, m, summed(left + m))
                return carry

            lax.fori_loop(0, left, onward, 0)
            finish(p, k + 1)
            copy_of(p, k + 1).start()

            def kept(m, carry):
                acc[m, own, :] = summed(m)
                return carry

            lax.fori_loop(0, left, kept, 0)
        else:
            total[own, :] = summed(0)
    out_ref[...] = total[...].T
    for k, p in steps:
        if (p, k) not in waited:
            copy_of(p, k).wait_send()


def whole_gradient(count, hidden_rows, weights, positive, wanted, negative):
    rows, depth = hidden_rows.shape
    columns = weights.shape[1]
    slots = wanted.shape[1]
    bits = count.bit_length() - 1
    plan = part_plan(columns, bits)
    parts = len(plan)
    message_rows = row_starts(count, plan)[2]
    chunks = 8
    width = depth // count
    slot_buffer = VMEM((count, slots // count, 128), jnp.bfloat16)
    return pl.pallas_call(
        functools.partial(whole_kernel, count, plan),
        out_shape=jax.ShapeDtypeStruct((width, columns), jnp.float32),
        in_specs=[pl.BlockSpec(memory_space=pl.ANY)] * 2 + [pl.BlockSpec(memory_space=VMEM)] * 3,
        out_specs=pl.BlockSpec(memory_space=VMEM),
        scratch_shapes=[
            VMEM((rows, depth), jnp.bfloat16),
            VMEM((depth, columns), jnp.float32),
            VMEM((rows, columns), jnp.float32),
            VMEM((rows, 1), jnp.float32),
            VMEM((rows, columns), jnp.bfloat16),
            VMEM((rows, columns), jnp.bfloat16),
            VMEM((rows, rows), jnp.bfloat16),
            VMEM((rows, rows), jnp.bfloat16),
            VMEM((rows, columns), jnp.float32),
            slot_buffer,
            slot_buffer,
            pltpu.SemaphoreType.DMA((2, chunks)),
            pltpu.SemaphoreType.DMA((4,)),
            pltpu.SemaphoreType.DMA((count,)),
            pltpu.SemaphoreType.DMA((count,)),
            VMEM((2 * columns, rows), jnp.bfloat16),
            VMEM((count // 2, columns, width), jnp.float32),
            VMEM((columns, width), jnp.float32),
            VMEM((16, width), jnp.float32),
            VMEM((16, width), jnp.float32),
            VMEM((message_rows, width), jnp.int16),
            VMEM((message_rows, width), jnp.int16),
            pltpu.SemaphoreType.DMA((parts, bits)),
            pltpu.SemaphoreType.DMA((parts, bits)),
        ],
        compiler_params=pltpu.CompilerParams(
            collective_id=0, has_side_effects=True, vmem_limit_bytes=54 * 1024 * 1024
        ),
        cost_estimate=pl.CostEstimate(
            flops=10 * rows * depth * columns, bytes_accessed=12 * rows * depth, transcendentals=0
        ),
    )(hidden_rows, weights, positive, wanted, negative)


def shards(hidden, head, pos_local, requests, neg_slot):
    hidden_rows = hidden[0]
    weights = head[0]
    row_count, depth = hidden_rows.shape
    shard_count = lax.axis_size("shard")
    slot_count = requests.shape[2]
    neg_count = neg_slot.shape[1]
    slot_total = shard_count * slot_count
    power_of_two = shard_count & (shard_count - 1) == 0 and shard_count > 1
    lane_groups = weights.shape[1] // 128
    if power_of_two and (depth // shard_count) % 128 == 0 and slot_count * lane_groups == 16:
        wanted = jnp.broadcast_to(requests, (shard_count, lane_groups, slot_count))
        return whole_gradient(
            shard_count, hidden_rows, weights, pos_local[:, None], wanted.reshape(1, -1), neg_slot
        )[None]
    embedded = jnp.dot(
        hidden_rows, weights, precision=lax.Precision.HIGHEST, preferred_element_type=jnp.float32
    )
    magnitude = jnp.sqrt(jnp.sum(embedded * embedded, axis=1, keepdims=True) + epsilon)
    unit_rows = embedded / magnitude
    normalized = unit_rows.astype(jnp.bfloat16)
    wanted_rows = requests[:, 0, :]
    flat_wanted = wanted_rows.reshape(-1)
    row_ids = jnp.arange(row_count, dtype=jnp.int32)
    owner_table = (row_ids[:, None] == flat_wanted[None, :]).astype(jnp.bfloat16)
    picked = lax.dot_general(
        owner_table, normalized, (((0,), (0,)), ((), ())), preferred_element_type=jnp.float32
    ).astype(jnp.bfloat16)
    sent_rows = lax.all_to_all(
        picked.reshape(shard_count, slot_count, -1),
        "shard",
        split_axis=0,
        concat_axis=0,
        tiled=True,
    )
    joined_rows = jnp.concatenate([normalized, sent_rows.reshape(slot_total, -1)], axis=0)
    arrived_rows = passed_along(joined_rows, "tower", -1)
    scores = jnp.exp(
        jnp.einsum("ot,bt->ob", normalized, arrived_rows, preferred_element_type=jnp.float32)
        / logit_divisor
        - logit_shift
    )
    slot_ids = jnp.arange(slot_total, dtype=jnp.int32)[None, :]
    slot_uses = jnp.zeros((row_count, slot_total), jnp.float32)
    for column in range(neg_count):
        slot_uses = slot_uses + (neg_slot[:, column : column + 1] == slot_ids).astype(jnp.float32)
    cobatch, mined = scores[:, :row_count], scores[:, row_count:]
    total = jnp.sum(cobatch, axis=1, keepdims=True) + jnp.sum(
        mined * slot_uses, axis=1, keepdims=True
    )
    target = (pos_local[:, None] == row_ids[None, :]).astype(jnp.float32)
    dlog = (cobatch / total - target).astype(jnp.bfloat16)
    slot_weight = slot_uses * lax.reduce_precision(mined / total, 8, 7)
    query_grad = (
        jnp.dot(dlog, arrived_rows[:row_count], preferred_element_type=jnp.float32)
        + jnp.dot(
            slot_weight,
            arrived_rows[row_count:].astype(jnp.float32),
            precision=lax.Precision.HIGHEST,
        )
    ) / logit_divisor
    passage_grad = (
        jnp.einsum("en,er->nr", dlog, normalized, preferred_element_type=jnp.float32)
        / logit_divisor
    )
    slot_grad = (
        jnp.dot(slot_weight.T, normalized.astype(jnp.float32), precision=lax.Precision.HIGHEST)
        / logit_divisor
    )
    joined_grads = jnp.concatenate([passage_grad, slot_grad], axis=0)
    arrived_grads = passed_along(joined_grads, "tower", 1)
    got_inbatch = arrived_grads[:row_count]
    got_slots = arrived_grads[row_count:].reshape(shard_count, slot_count, -1)
    returned_slots = lax.all_to_all(
        got_slots.astype(jnp.bfloat16), "shard", split_axis=0, concat_axis=0, tiled=True
    )
    returned = got_inbatch + jnp.dot(
        owner_table, returned_slots.reshape(slot_total, -1), preferred_element_type=jnp.float32
    )
    is_query = lax.axis_index("tower") == 0
    d_unit = jnp.where(is_query, query_grad, returned)
    d_embedded = (
        d_unit - unit_rows * jnp.sum(unit_rows * d_unit, axis=1, keepdims=True)
    ) / magnitude
    head_grad = lax.psum_scatter(
        jnp.einsum(
            "rd,rp->dp",
            hidden_rows,
            d_embedded,
            precision=lax.Precision.HIGHEST,
            preferred_element_type=jnp.float32,
        ),
        "shard",
        scatter_dimension=0,
        tiled=True,
    )
    return head_grad[None]


def solution(mesh):
    placed = (
        P("tower", "shard", None),
        P("tower", None, None),
        P("shard"),
        P(None, "shard", None),
        P("shard", None),
    )
    return jax.shard_map(
        shards, mesh=mesh, in_specs=placed, out_specs=P("tower", "shard", None), check_vma=False
    )
```

```python
import functools

import jax
import jax.numpy as jnp
from jax import lax
from jax.experimental import pallas as pl
from jax.experimental.pallas import tpu as pltpu
from jax.sharding import PartitionSpec as P

logit_divisor = 0.05
logit_shift = 20.0
epsilon = 1e-06
code_steps = 128.0
code_range = 32700.0
PIECES, STAGGER, UNROLL = 2, False, 2
least_value = 1e-30
MESH = pl.DeviceIdType.MESH
VMEM = pltpu.VMEM


def passed_along(block, axis, distance):
    devices = range(lax.axis_size(axis))
    route = [(i - distance, i) for i in devices if i - distance in devices]
    return lax.ppermute(block, axis, route)


def part_plan(columns, bits):
    low = list(range(bits))
    if bits < 3:
        return [(columns // 2, low)] * 2
    rest = low[3:]
    orders = ([0, 1, 2] + rest, [1, 2, 0] + rest, [2, 0, 1] + rest)
    piece = columns // PIECES
    wide = (piece * 11 // 32 + 15) // 16 * 16
    sizes = [wide, wide, piece - 2 * wide]
    return [(size, order) for _ in range(PIECES) for size, order in zip(sizes, orders)]


def front(
    count,
    hidden_hbm,
    head_hbm,
    positive_ref,
    wanted_ref,
    negative_ref,
    hidden_ref,
    head_ref,
    unit_ref,
    scale_ref,
    unit_b_ref,
    mate_ref,
    dlog_ref,
    dlog_got_ref,
    grad_ref,
    slots_out_ref,
    slots_in_ref,
    load_sem,
    pair_sem,
    slot_send_sem,
    slot_recv_sem,
    greet,
):
    tower = lax.axis_index("tower")
    me = lax.axis_index("shard")
    rows, depth = hidden_ref.shape
    columns = unit_ref.shape[1]
    chunks = load_sem.shape[1]
    chunk = depth // chunks
    slots = count * slots_in_ref.shape[1]
    lane_groups = columns // 128
    picks = slots // (count * lane_groups)
    per_owner = picks * lane_groups

    def loads(c):
        span = pl.ds(c * chunk, chunk)
        return (
            pltpu.make_async_copy(hidden_hbm.at[:, span], hidden_ref.at[:, span], load_sem.at[0, c]),
            pltpu.make_async_copy(head_hbm.at[span, :], head_ref.at[span, :], load_sem.at[1, c]),
        )

    def to_mate(source, target, which):
        return pltpu.make_async_remote_copy(
            src_ref=source,
            dst_ref=target,
            send_sem=pair_sem.at[which],
            recv_sem=pair_sem.at[which + 1],
            device_id=(1 - tower, me),
            device_id_type=MESH,
        )

    def slot_copy(i):
        other = lax.rem(me + i, count)
        return pltpu.make_async_remote_copy(
            src_ref=slots_out_ref.at[other],
            dst_ref=slots_in_ref.at[me],
            send_sem=slot_send_sem.at[i],
            recv_sem=slot_recv_sem.at[me],
            device_id=(1 - tower, other),
            device_id_type=MESH,
        )

    def slots_arrive():
        for o in range(count):
            pltpu.make_async_remote_copy(
                src_ref=slots_out_ref.at[o],
                dst_ref=slots_in_ref.at[o],
                send_sem=slot_send_sem.at[o],
                recv_sem=slot_recv_sem.at[o],
                device_id=(1 - tower, me),
                device_id_type=MESH,
            ).wait_recv()

    def dot(left, right, dims):
        return lax.dot_general(left, right, (dims, ((), ())), preferred_element_type=jnp.float32)

    def group_of(shape, axis):
        return (lax.broadcasted_iota(jnp.int32, shape, axis) >> (picks.bit_length() - 1)) & (
            lane_groups - 1
        )

    def send_slots(table):
        group = group_of((slots, 128), 0)
        packed = jnp.zeros((slots, 128), jnp.float32)
        for q in range(lane_groups):
            packed = packed + jnp.where(group == q, table[:, q * 128 : (q + 1) * 128], 0.0)
        packed = packed.astype(jnp.bfloat16)
        for o in range(count):
            slots_out_ref[o] = packed[o * per_owner : (o + 1) * per_owner, :]
        for i in range(count):
            slot_copy(i).start()

    def read_slots():
        packed = jnp.concatenate([slots_in_ref[o] for o in range(count)], axis=0)
        row = lax.broadcasted_iota(jnp.int32, (slots, slots), 0)
        column = lax.broadcasted_iota(jnp.int32, (slots, slots), 1)
        low, high = picks - 1, -per_owner
        same = ((row & low) == (column & low)) & ((row & high) == (column & high))
        group = group_of((slots, slots), 1)
        pieces = []
        for q in range(lane_groups):
            chosen = (same & (group == q)).astype(jnp.float32).astype(jnp.bfloat16)
            pieces.append(dot(chosen, packed, ((1,), (0,))).astype(jnp.bfloat16))
        return jnp.concatenate(pieces, axis=1)

    for c in range(chunks):
        for load in loads(c):
            load.start()
    for c in range(chunks):
        for load in loads(c):
            load.wait()
        span = slice(c * chunk, (c + 1) * chunk)
        weights = head_ref[span, :]
        first = weights.astype(jnp.bfloat16)
        left = weights - first.astype(jnp.float32)
        second = left.astype(jnp.bfloat16)
        third = (left - second.astype(jnp.float32)).astype(jnp.bfloat16)
        block = hidden_ref[:, span]
        term = (
            dot(block, third, ((1,), (0,)))
            + dot(block, second, ((1,), (0,)))
            + dot(block, first, ((1,), (0,)))
        )
        if c == 0:
            unit_ref[...] = term
        else:
            unit_ref[...] += term
    embedded = unit_ref[...]
    inverse = 1.0 / jnp.sqrt(jnp.sum(embedded * embedded, axis=1, keepdims=True) + epsilon)
    unit = embedded * inverse
    unit_ref[...] = unit
    scale_ref[...] = inverse
    unit_b_ref[...] = unit.astype(jnp.bfloat16)
    greet()
    to_mate(unit_b_ref, mate_ref, 0).start()
    lane_owner = lax.broadcasted_iota(jnp.int32, (rows, slots), 0) == wanted_ref[...]

    @pl.when(tower == 1)
    def _():
        table = lane_owner.astype(jnp.float32).astype(jnp.bfloat16)
        send_slots(dot(table, unit_b_ref[...], ((0,), (0,))))
        to_mate(unit_b_ref, mate_ref, 0).wait_recv()
        to_mate(dlog_ref, dlog_got_ref, 2).wait_recv()
        grad_ref[...] = dot(dlog_got_ref[...], mate_ref[...], ((0,), (0,))) / logit_divisor
        slots_arrive()
        once = lane_owner & (group_of((rows, slots), 1) == 0)
        grad_ref[...] += dot(
            once.astype(jnp.float32).astype(jnp.bfloat16), read_slots(), ((1,), (0,))
        )

    @pl.when(tower == 0)
    def _():
        lane = lax.broadcasted_iota(jnp.int32, (rows, slots), 1)
        slot_id = (lane >> (per_owner.bit_length() - 1)) * picks + (lane & (picks - 1))
        uses = jnp.zeros((rows, slots), jnp.float32)
        for k in range(negative_ref.shape[1]):
            uses = uses + (negative_ref[:, k : k + 1] == slot_id).astype(jnp.float32)
        once = (group_of((rows, slots), 1) == 0).astype(jnp.float32)
        to_mate(unit_b_ref, mate_ref, 0).wait_recv()
        cobatch = jnp.exp(
            dot(unit_b_ref[...], mate_ref[...], ((1,), (1,))) / logit_divisor - logit_shift
        )
        cobatch_sum = jnp.sum(cobatch, axis=1, keepdims=True)
        slots_arrive()
        pulled = read_slots()
        mined = jnp.exp(
            dot(unit_b_ref[...], pulled, ((1,), (1,))) / logit_divisor - logit_shift
        )
        share = 1.0 / (cobatch_sum + jnp.sum(mined * uses * once, axis=1, keepdims=True))
        target = lax.broadcasted_iota(jnp.int32, (rows, rows), 1) == positive_ref[...]
        dlog_ref[...] = (cobatch * share - target.astype(jnp.float32)).astype(jnp.bfloat16)
        to_mate(dlog_ref, dlog_got_ref, 2).start()
        weight = uses * (mined * share).astype(jnp.bfloat16).astype(jnp.float32)
        upper = weight.astype(jnp.bfloat16)
        lower = (weight - upper.astype(jnp.float32)).astype(jnp.bfloat16)
        slot_grad = dot(upper, unit_b_ref[...], ((0,), (0,))) + dot(
            lower, unit_b_ref[...], ((0,), (0,))
        )
        send_slots(slot_grad / logit_divisor)
        once_b = once.astype(jnp.bfloat16)
        grad_ref[...] = (
            dot(dlog_ref[...], mate_ref[...], ((1,), (0,)))
            + dot(upper * once_b, pulled, ((1,), (0,)))
            + dot(lower * once_b, pulled, ((1,), (0,)))
        ) / logit_divisor
        to_mate(dlog_ref, dlog_got_ref, 2).wait_send()

    d_unit, unit = grad_ref[...], unit_ref[...]
    along = jnp.sum(unit * d_unit, axis=1, keepdims=True)
    grad_ref[...] = (d_unit - unit * along) * scale_ref[...]
    to_mate(unit_b_ref, mate_ref, 0).wait_send()
    for i in range(count):
        slot_copy(i).wait_send()


def row_starts(count, plan):
    starts, messages, column, row = [], {}, 0, 0
    for p, (part, order) in enumerate(plan):
        starts.append(column)
        column += part
        for k in range(len(order)):
            messages[p, k] = row
            row += (count >> (k + 1)) * part + 16
    return starts, messages, row


def whole_kernel(
    count, plan, hidden_hbm, head_hbm, positive_ref, wanted_ref, negative_ref, out_ref, *scratch
):
    bits = len(plan[0][1])
    parts = len(plan)
    starts, messages, _ = row_starts(count, plan)
    half = count // 2
    hidden_ref, d_ref = scratch[0], scratch[8]
    front_refs, scratch = scratch[:15], scratch[15:]
    rows, depth = hidden_ref.shape
    width = depth // count
    terms, acc, total, codes, scales, sent, got, send_sem, recv_sem = scratch
    tower = lax.axis_index("tower")
    me = lax.axis_index("shard")

    def bit_of(number, b):
        return (number // (1 << b)) % 2

    def partner(b):
        return me + (1 - 2 * bit_of(me, b)) * (1 << b)

    barrier = pltpu.get_barrier_semaphore()
    for b in range(bits):
        pl.semaphore_signal(barrier, inc=1, device_id=(tower, partner(b)), device_id_type=MESH)
    for o in range(count):
        pl.semaphore_signal(barrier, inc=1, device_id=(1 - tower, o), device_id_type=MESH)

    def greet():
        pl.semaphore_wait(barrier, bits + count)

    front(count, hidden_hbm, head_hbm, positive_ref, wanted_ref, negative_ref, *front_refs, greet)
    turned = d_ref[...].T
    upper = turned.astype(jnp.bfloat16)
    lower = (turned - upper.astype(jnp.float32)).astype(jnp.bfloat16)
    for p, (part, _) in enumerate(plan):
        start = starts[p]
        terms[2 * start : 2 * start + part, :] = upper[start : start + part, :]
        terms[2 * start + part : 2 * (start + part), :] = lower[start : start + part, :]

    def product(p, m, leading):
        part, order = plan[p]
        block = 0
        for t, b in enumerate(order):
            if t == 0:
                own = (bit_of(me, b) + leading) % 2
            else:
                own = (bit_of(me, b) + bit_of(m, bits - 1 - t)) % 2
            block = block + own * (1 << b)
        columns = pl.ds(pl.multiple_of(block * width, width), width)
        both = jnp.dot(
            terms[2 * starts[p] : 2 * (starts[p] + part), :],
            hidden_ref[:, columns],
            preferred_element_type=jnp.float32,
        )
        return both[:part] + both[part:]

    def encode(p, k, m, value):
        part = plan[p][0]
        largest = jnp.maximum(jnp.max(jnp.abs(value), axis=0, keepdims=True), least_value)
        code = jnp.ceil(jnp.log2(largest) * code_steps)
        scaled = value * (jnp.exp2(code * (-1.0 / code_steps)) * code_range)
        whole = jnp.round(scaled).astype(jnp.int32).astype(jnp.int16)
        sent[pl.ds(pl.multiple_of(messages[p, k] + m * part, 16), part), :] = whole
        codes[pl.ds(m, 1), :] = code

    def copy_of(p, k):
        part, order = plan[p]
        span = pl.ds(messages[p, k], (count >> (k + 1)) * part + 16)
        return pltpu.make_async_remote_copy(
            src_ref=sent.at[span, :],
            dst_ref=got.at[span, :],
            send_sem=send_sem.at[p, k],
            recv_sem=recv_sem.at[p, k],
            device_id=(tower, partner(order[k])),
            device_id_type=MESH,
        )

    def finish(p, k):
        end = messages[p, k] + (count >> (k + 1)) * plan[p][0]
        sent[end : end + 16, :] = codes[...].astype(jnp.int32).astype(jnp.int16)

    codes[...] = jnp.zeros_like(codes)
    for p in range(parts):

        def first_half(m, carry):
            encode(p, 0, m, product(p, m, 1))
            return carry

        lax.fori_loop(0, half, first_half, 0, unroll=UNROLL)
        finish(p, 0)
        if not STAGGER or p < parts // PIECES:
            copy_of(p, 0).start()
    for p, (part, _) in enumerate(plan):

        def second_half(m, carry):
            acc[m, starts[p] : starts[p] + part, :] = product(p, m, 0)
            return carry

        lax.fori_loop(0, half, second_half, 0, unroll=UNROLL)
    waited = set()
    if STAGGER:
        for p in range(parts // PIECES, parts):
            copy_of(p - parts // PIECES, 0).wait_send()
            waited.add((p - parts // PIECES, 0))
            copy_of(p, 0).start()

    steps = [(k, p) for k in range(bits) for p in range(parts)]
    if STAGGER:
        lead = parts // PIECES
        steps = sorted(steps, key=lambda step: (step[0] + step[1] // lead, step[1]))
    for k, p in steps:
        part = plan[p][0]
        blocks = count >> (k + 1)
        left = blocks // 2
        own = slice(starts[p], starts[p] + part)
        copy_of(p, k).wait_recv()
        end = messages[p, k] + blocks * part
        scales[...] = jnp.exp2(
            got[end : end + 16, :].astype(jnp.int32).astype(jnp.float32) * (1.0 / code_steps)
        ) * (1.0 / code_range)

        def summed(m):
            coded = got[pl.ds(pl.multiple_of(messages[p, k] + m * part, 16), part), :]
            value = coded.astype(jnp.int32).astype(jnp.float32)
            return acc[m, own, :] + value * scales[pl.ds(m, 1), :]

        if k + 1 < bits:

            def onward(m, carry):
                encode(p, k + 1, m, summed(left + m))
                return carry

            lax.fori_loop(0, left, onward, 0, unroll=min(left, 2))
            finish(p, k + 1)
            copy_of(p, k + 1).start()

            def kept(m, carry):
                acc[m, own, :] = summed(m)
                return carry

            lax.fori_loop(0, left, kept, 0, unroll=min(left, 2))
        else:
            total[own, :] = summed(0)
    out_ref[...] = total[...].T
    for k, p in steps:
        if (p, k) not in waited:
            copy_of(p, k).wait_send()


def whole_gradient(count, hidden_rows, weights, positive, wanted, negative):
    rows, depth = hidden_rows.shape
    columns = weights.shape[1]
    slots = wanted.shape[1]
    bits = count.bit_length() - 1
    plan = part_plan(columns, bits)
    parts = len(plan)
    message_rows = row_starts(count, plan)[2]
    chunks = 8
    width = depth // count
    slot_buffer = VMEM((count, slots // count, 128), jnp.bfloat16)
    return pl.pallas_call(
        functools.partial(whole_kernel, count, plan),
        out_shape=jax.ShapeDtypeStruct((width, columns), jnp.float32),
        in_specs=[pl.BlockSpec(memory_space=pl.ANY)] * 2 + [pl.BlockSpec(memory_space=VMEM)] * 3,
        out_specs=pl.BlockSpec(memory_space=VMEM),
        scratch_shapes=[
            VMEM((rows, depth), jnp.bfloat16),
            VMEM((depth, columns), jnp.float32),
            VMEM((rows, columns), jnp.float32),
            VMEM((rows, 1), jnp.float32),
            VMEM((rows, columns), jnp.bfloat16),
            VMEM((rows, columns), jnp.bfloat16),
            VMEM((rows, rows), jnp.bfloat16),
            VMEM((rows, rows), jnp.bfloat16),
            VMEM((rows, columns), jnp.float32),
            slot_buffer,
            slot_buffer,
            pltpu.SemaphoreType.DMA((2, chunks)),
            pltpu.SemaphoreType.DMA((4,)),
            pltpu.SemaphoreType.DMA((count,)),
            pltpu.SemaphoreType.DMA((count,)),
            VMEM((2 * columns, rows), jnp.bfloat16),
            VMEM((count // 2, columns, width), jnp.float32),
            VMEM((columns, width), jnp.float32),
            VMEM((16, width), jnp.float32),
            VMEM((16, width), jnp.float32),
            VMEM((message_rows, width), jnp.int16),
            VMEM((message_rows, width), jnp.int16),
            pltpu.SemaphoreType.DMA((parts, bits)),
            pltpu.SemaphoreType.DMA((parts, bits)),
        ],
        compiler_params=pltpu.CompilerParams(
            collective_id=0, has_side_effects=True, vmem_limit_bytes=54 * 1024 * 1024
        ),
        cost_estimate=pl.CostEstimate(
            flops=10 * rows * depth * columns, bytes_accessed=12 * rows * depth, transcendentals=0
        ),
    )(hidden_rows, weights, positive, wanted, negative)


def shards(hidden, head, pos_local, requests, neg_slot):
    hidden_rows = hidden[0]
    weights = head[0]
    row_count, depth = hidden_rows.shape
    shard_count = lax.axis_size("shard")
    slot_count = requests.shape[2]
    neg_count = neg_slot.shape[1]
    slot_total = shard_count * slot_count
    power_of_two = shard_count & (shard_count - 1) == 0 and shard_count > 1
    lane_groups = weights.shape[1] // 128
    if power_of_two and (depth // shard_count) % 128 == 0 and slot_count * lane_groups == 16:
        wanted = jnp.broadcast_to(requests, (shard_count, lane_groups, slot_count))
        return whole_gradient(
            shard_count, hidden_rows, weights, pos_local[:, None], wanted.reshape(1, -1), neg_slot
        )[None]
    embedded = jnp.dot(
        hidden_rows, weights, precision=lax.Precision.HIGHEST, preferred_element_type=jnp.float32
    )
    magnitude = jnp.sqrt(jnp.sum(embedded * embedded, axis=1, keepdims=True) + epsilon)
    unit_rows = embedded / magnitude
    normalized = unit_rows.astype(jnp.bfloat16)
    wanted_rows = requests[:, 0, :]
    flat_wanted = wanted_rows.reshape(-1)
    row_ids = jnp.arange(row_count, dtype=jnp.int32)
    owner_table = (row_ids[:, None] == flat_wanted[None, :]).astype(jnp.bfloat16)
    picked = lax.dot_general(
        owner_table, normalized, (((0,), (0,)), ((), ())), preferred_element_type=jnp.float32
    ).astype(jnp.bfloat16)
    sent_rows = lax.all_to_all(
        picked.reshape(shard_count, slot_count, -1),
        "shard",
        split_axis=0,
        concat_axis=0,
        tiled=True,
    )
    joined_rows = jnp.concatenate([normalized, sent_rows.reshape(slot_total, -1)], axis=0)
    arrived_rows = passed_along(joined_rows, "tower", -1)
    scores = jnp.exp(
        jnp.einsum("ot,bt->ob", normalized, arrived_rows, preferred_element_type=jnp.float32)
        / logit_divisor
        - logit_shift
    )
    slot_ids = jnp.arange(slot_total, dtype=jnp.int32)[None, :]
    slot_uses = jnp.zeros((row_count, slot_total), jnp.float32)
    for column in range(neg_count):
        slot_uses = slot_uses + (neg_slot[:, column : column + 1] == slot_ids).astype(jnp.float32)
    cobatch, mined = scores[:, :row_count], scores[:, row_count:]
    total = jnp.sum(cobatch, axis=1, keepdims=True) + jnp.sum(
        mined * slot_uses, axis=1, keepdims=True
    )
    target = (pos_local[:, None] == row_ids[None, :]).astype(jnp.float32)
    dlog = (cobatch / total - target).astype(jnp.bfloat16)
    slot_weight = slot_uses * lax.reduce_precision(mined / total, 8, 7)
    query_grad = (
        jnp.dot(dlog, arrived_rows[:row_count], preferred_element_type=jnp.float32)
        + jnp.dot(
            slot_weight,
            arrived_rows[row_count:].astype(jnp.float32),
            precision=lax.Precision.HIGHEST,
        )
    ) / logit_divisor
    passage_grad = (
        jnp.einsum("en,er->nr", dlog, normalized, preferred_element_type=jnp.float32)
        / logit_divisor
    )
    slot_grad = (
        jnp.dot(slot_weight.T, normalized.astype(jnp.float32), precision=lax.Precision.HIGHEST)
        / logit_divisor
    )
    joined_grads = jnp.concatenate([passage_grad, slot_grad], axis=0)
    arrived_grads = passed_along(joined_grads, "tower", 1)
    got_inbatch = arrived_grads[:row_count]
    got_slots = arrived_grads[row_count:].reshape(shard_count, slot_count, -1)
    returned_slots = lax.all_to_all(
        got_slots.astype(jnp.bfloat16), "shard", split_axis=0, concat_axis=0, tiled=True
    )
    returned = got_inbatch + jnp.dot(
        owner_table, returned_slots.reshape(slot_total, -1), preferred_element_type=jnp.float32
    )
    is_query = lax.axis_index("tower") == 0
    d_unit = jnp.where(is_query, query_grad, returned)
    d_embedded = (
        d_unit - unit_rows * jnp.sum(unit_rows * d_unit, axis=1, keepdims=True)
    ) / magnitude
    head_grad = lax.psum_scatter(
        jnp.einsum(
            "rd,rp->dp",
            hidden_rows,
            d_embedded,
            precision=lax.Precision.HIGHEST,
            preferred_element_type=jnp.float32,
        ),
        "shard",
        scatter_dimension=0,
        tiled=True,
    )
    return head_grad[None]


def solution(mesh):
    placed = (
        P("tower", "shard", None),
        P("tower", None, None),
        P("shard"),
        P(None, "shard", None),
        P("shard", None),
    )
    return jax.shard_map(
        shards, mesh=mesh, in_specs=placed, out_specs=P("tower", "shard", None), check_vma=False
    )
```
